32 devices in a mesh: groups: 2 (over y), seq: 8 (over z, core), panel: 2 (over x).
Axes of the slice: x: 2, y: 2, z: 4, core: 2. Of those that a mesh axis runs over, the one named last changes fastest.
Arguments:
- queries: bfloat16 [4096, 3072], P(('groups', 'seq'), 'panel'), parts along dimension 0, may hold values from -120 to 120
- key_rows: bfloat16 [4096, 3072], P(('groups', 'seq'), 'panel'), parts along dimension 0, may hold values from -6 to 6
- value_rows: bfloat16 [4096, 3072], P(('groups', 'seq'), 'panel'), parts along dimension 0, may hold values from -6 to 6
- block_lists: int32 [24, 16, 8], P('panel'), may hold values from 0 to 15, as said below
- block_counts: int32 [24, 16], P('panel'), may hold values from 4 to 8, as said below
Outputs:
- attended: bfloat16 [4096, 3072], P(('groups', 'seq', 'panel')), parts along dimension 0
The draws below stay inside these ranges and needn't reach their ends.
There are 2 independent parts, one for each index of `groups`. The reference program is written for one: setup_inputs(seed, part) draws one part's arguments, and reference() takes and returns one part's arrays. A program takes and returns all parts, laid end to end along the dimension named above; an argument that names none is the same for every part. Nothing has to cross between parts.
Inputs may be any that keep to these rules, and one draw needn't show every extreme that they name: `block_lists`: entry 0 of each list is the tile's own block index; the entries of one list are distinct; for each head, the lists of the 2 tiles held by one index of seq name together at most 1 distinct blocks among the 2 blocks of any other index of seq, and exactly 1 of some other index. `block_counts`: some list has all 8 entries live.
All inputs are finite; a program needn't handle non-finite values.
Results may differ from the reference program's by a relative error of at most 0.008.
Values may be sent and summed in bfloat16 or wider, within the bound.
A program may use at most 128 MiB of HBM per device.

```python
import jax
import jax.numpy as jnp
from jax import lax

HEADS = 24
HEAD_DIM = 128
BLOCK = 128
TOK_DEV = 256
TOKENS = 2048
TILES = 16
LISTED = 8
SLOTS = 1


def query_key_pair(key):
    base = jax.random.fold_in(key, 7)
    key_part = jax.random.normal(jax.random.fold_in(base, 1), (TOKENS, HEADS * HEAD_DIM), jnp.float32)
    key_part = jnp.clip(key_part, -5.0, 5.0)
    query_part = jnp.clip(jax.random.normal(jax.random.fold_in(base, 2), (TOKENS, HEADS * HEAD_DIM), jnp.float32), -5.0, 5.0)
    return (query_part, key_part)


def draw_queries(key, part):
    return query_key_pair(key)[0].astype(jnp.bfloat16)


def draw_key_rows(key, part):
    return query_key_pair(key)[1].astype(jnp.bfloat16)


def draw_block_lists(key, part):
    base = jax.random.fold_in(key, 11)
    owned = TOK_DEV // BLOCK
    peers = TILES // owned
    width = owned + SLOTS * (peers - 1)
    pick_bits = jax.random.randint(jax.random.fold_in(base, 1), (HEADS, peers, peers, owned), 0, 1 << 20)
    pick_scores = pick_bits * owned + jnp.arange(owned, dtype=jnp.int32)[None, None, None, :]
    picked = jnp.argsort(pick_scores, axis=-1)[..., :SLOTS].astype(jnp.int32)
    chosen = picked + (jnp.arange(peers, dtype=jnp.int32) * owned)[None, None, :, None]
    peer_rows = jnp.arange(peers, dtype=jnp.int32)
    other_index = jnp.arange(peers - 1, dtype=jnp.int32)[None, :] + (jnp.arange(peers - 1, dtype=jnp.int32)[None, :] >= peer_rows[:, None]).astype(jnp.int32)
    others = jnp.take_along_axis(chosen, jnp.broadcast_to(other_index[None, :, :, None], (HEADS, peers, peers - 1, SLOTS)), axis=2)
    others = others.reshape(HEADS, peers, (peers - 1) * SLOTS)
    own_ids = peer_rows[:, None] * owned + jnp.arange(owned, dtype=jnp.int32)[None, :]
    candidates = jnp.concatenate([jnp.broadcast_to(own_ids[None], (HEADS, peers, owned)), others], axis=-1)
    per_tile = jnp.repeat(candidates, owned, axis=1)
    tile_ids = jnp.arange(TILES, dtype=jnp.int32)
    place = tile_ids % owned
    device = tile_ids // owned
    spots = jnp.arange(width - 1, dtype=jnp.int32)
    keep_index = spots[None, :] + (spots[None, :] >= place[:, None]).astype(jnp.int32)
    rest = jnp.take_along_axis(per_tile, jnp.broadcast_to(keep_index[None], (HEADS, TILES, width - 1)), axis=2)
    bits = jax.random.randint(jax.random.fold_in(base, 2), (HEADS, TILES, width - 1), 0, 1 << 20)
    scores = (bits + 1) * width + spots[None, None, :]
    favored_peer = jnp.where(device == peers - 1, 0, device)
    first_spot = owned - 1 + favored_peer * SLOTS
    favored = (spots[None, :] >= first_spot[:, None]) & (spots[None, :] < first_spot[:, None] + SLOTS) & (place[:, None] == 0)
    scores = jnp.where(favored[None], jnp.broadcast_to(spots[None, None, :], scores.shape), scores)
    order = jnp.argsort(scores, axis=-1)[:, :, :LISTED - 1].astype(jnp.int32)
    rest_taken = jnp.take_along_axis(rest, order, axis=2)
    own = jnp.broadcast_to(tile_ids[None, :, None], (HEADS, TILES, 1))
    return jnp.concatenate([own, rest_taken], axis=-1).astype(jnp.int32)


def draw_block_counts(key, part):
    base = jax.random.fold_in(key, 13)
    counts = jax.random.randint(base, (HEADS, TILES), LISTED // 2, LISTED + 1)
    head_pick = jax.random.randint(jax.random.fold_in(base, 1), (), 0, HEADS)
    tile_pick = jax.random.randint(jax.random.fold_in(base, 2), (), 0, TILES)
    return counts.at[head_pick, tile_pick].set(LISTED).astype(jnp.int32)


def levels(stream_key, extent, cuts, low, top_value):
    factor_of, own = 1.0, jax.random.fold_in(stream_key, 6)
    for axis_at, parts in cuts:
        draws = jnp.exp(jax.random.uniform(jax.random.fold_in(own, axis_at), (parts,), jnp.float32, low / len(cuts), top_value / len(cuts)))
        factor_of = factor_of * jnp.repeat(draws, extent[axis_at] // parts).reshape([-1 if axis == axis_at else 1 for axis in range(len(extent))])
    return factor_of


def bell_draw(stream_key, shape, deviation, bound, shards=(), kind=jnp.bfloat16):
    values = jax.random.normal(stream_key, shape, jnp.float32) * deviation
    if len(shards) > 0:
        values = levels(stream_key, shape, shards, -0.22, 0.18) * values
    return jnp.clip(values, min=-bound, max=bound).astype(kind)


def setup_inputs(seed: int = 0, part: int = 0) -> dict:
    key_list = jax.random.split(jax.random.key(seed), 6)
    own_keys = jax.random.split(jax.random.fold_in(key_list[5], part), 6)
    queries = draw_queries(jax.random.fold_in(jax.random.fold_in(key_list[5], part), 71), part)
    key_rows = draw_key_rows(jax.random.fold_in(jax.random.fold_in(key_list[5], part), 71), part)
    value_rows = bell_draw(own_keys[2], (TOKENS, HEADS * HEAD_DIM), 1.0, 6.0, ((0, 8), (1, 2)))
    block_lists = draw_block_lists(jax.random.fold_in(key_list[5], 71), part)
    block_counts = draw_block_counts(jax.random.fold_in(key_list[5], 71), part)
    return dict(queries=queries, key_rows=key_rows, value_rows=value_rows, block_lists=block_lists, block_counts=block_counts)


def reference(queries, key_rows, value_rows, block_lists, block_counts):
    tiles = queries.shape[0] // BLOCK
    scale = HEAD_DIM ** -0.5
    query_four = queries.reshape(tiles, BLOCK, HEADS, HEAD_DIM)
    key_four = key_rows.reshape(tiles, BLOCK, HEADS, HEAD_DIM)
    value_four = value_rows.reshape(tiles, BLOCK, HEADS, HEAD_DIM)
    live = jnp.arange(LISTED, dtype=jnp.int32)[None, None, :] < block_counts[:, :, None]

    def one_head(head):
        query_head = lax.dynamic_index_in_dim(query_four, head, 2, keepdims=False)
        key_head = lax.dynamic_index_in_dim(key_four, head, 2, keepdims=False)
        value_head = lax.dynamic_index_in_dim(value_four, head, 2, keepdims=False)
        listed = lax.dynamic_index_in_dim(block_lists, head, 0, keepdims=False)
        live_head = lax.dynamic_index_in_dim(live, head, 0, keepdims=False)
        key_taken = jnp.take(key_head, listed, axis=0)
        value_taken = jnp.take(value_head, listed, axis=0)
        scores = jnp.einsum("tqd,tjkd->tqjk", query_head.astype(jnp.float32), key_taken.astype(jnp.float32)) * scale
        mask = live_head[:, None, :, None]
        masked = jnp.where(mask, scores, -1e30)
        top = jnp.max(masked, axis=(2, 3), keepdims=True)
        weights = jnp.where(mask, jnp.exp(masked - top), 0.0)
        total = jnp.sum(weights, axis=(2, 3))
        rounded = weights.astype(jnp.bfloat16)
        mixed = jnp.einsum("tqjk,tjkd->tqd", rounded.astype(jnp.float32), value_taken.astype(jnp.float32))
        return (mixed / total[:, :, None]).astype(jnp.bfloat16)

    results = lax.map(one_head, jnp.arange(HEADS, dtype=jnp.int32))
    return results.transpose(1, 2, 0, 3).reshape(tiles * BLOCK, HEADS * HEAD_DIM)
```

```python
import functools

import jax
import jax.numpy as jnp
from jax import lax
from jax.experimental import pallas as pl
from jax.experimental.pallas import tpu as pltpu
from jax.sharding import PartitionSpec as P

HEAD_DIM = 128
BLOCK = 128
CORES = 2
MESH = pl.DeviceIdType.MESH


def gathered(queries, key_rows, value_rows, block_lists, block_counts):
    local_rows = queries.shape[0]
    heads_here = queries.shape[1] // HEAD_DIM
    tiles_here = local_rows // BLOCK
    listed_len = block_lists.shape[2]
    scale = HEAD_DIM ** (-0.5)
    position = lax.axis_index("seq")
    my_lists = lax.dynamic_slice_in_dim(block_lists, position * tiles_here, tiles_here, 1)
    my_counts = lax.dynamic_slice_in_dim(block_counts, position * tiles_here, tiles_here, 1)
    slot_live = jnp.arange(listed_len, dtype=jnp.int32)[None, None, :] < my_counts[:, :, None]
    query_heads = queries.reshape(local_rows, heads_here, HEAD_DIM).transpose(1, 0, 2)
    key_piece = lax.all_gather(key_rows, "seq", axis=0, tiled=True)
    value_piece = lax.all_gather(value_rows, "seq", axis=0, tiled=True)
    piece_rows = key_piece.shape[0]
    piece_ids = jnp.arange(piece_rows // BLOCK, dtype=jnp.int32)
    hits = (my_lists[:, :, :, None] == piece_ids[None, None, None, :]) & slot_live[:, :, :, None]
    keep = jnp.any(hits, axis=2)
    key_heads = key_piece.reshape(piece_rows, heads_here, HEAD_DIM).transpose(1, 0, 2)
    value_heads = value_piece.reshape(piece_rows, heads_here, HEAD_DIM).transpose(1, 0, 2)

    def one_head(items):
        query_head, key_head, value_head, keep_head = items
        mask = jnp.repeat(jnp.repeat(keep_head, BLOCK, axis=0), BLOCK, axis=1)
        scores = (
            lax.dot_general(
                query_head, key_head, (((1,), (1,)), ((), ())), preferred_element_type=jnp.float32
            )
            * scale
        )
        masked = jnp.where(mask, scores, -1e30)
        top = jnp.max(masked, axis=1, keepdims=True)
        weights = jnp.where(mask, jnp.exp(masked - top), 0.0)
        total = jnp.sum(weights, axis=1, keepdims=True)
        mixed = jnp.dot(weights.astype(jnp.bfloat16), value_head, preferred_element_type=jnp.float32)
        return (mixed / total).astype(jnp.bfloat16)

    results = lax.map(one_head, (query_heads, key_heads, value_heads, keep))
    joined = results.transpose(1, 0, 2).reshape(local_rows, heads_here * HEAD_DIM)
    return lax.all_to_all(joined, "panel", split_axis=0, concat_axis=1, tiled=True)


def spread_kernel(
    n, panels, heads, trio,
    lists, counts, q, k, v, out,
    qf, kf, vf, qs, ks, vs, of, os,
    fsend, frecv, qsend, qrecv, csend, crecv, wsend, osend, orecv,
):
    me = lax.axis_index("seq")
    pan = lax.axis_index("panel")
    chip, core = me // CORES, me % CORES
    chips = n // CORES
    sibling = chip * CORES + 1 - core
    held = q.shape[0]
    listed = lists.shape[2]
    tiles = n * panels
    scale = HEAD_DIM ** (-0.5)
    flat = me * panels + pan

    def columns(head):
        return pl.ds(pl.multiple_of(head * HEAD_DIM, HEAD_DIM), HEAD_DIM)

    def span(at, size):
        return pl.ds(pl.multiple_of(at * size, size), size)

    def whole_head(device):
        return (device // CORES) * trio + device % CORES

    def shared_head(device):
        return (device // CORES) * trio + CORES

    def full_copy(kind, step, device):
        src, dst = ((k, kf), (q, qf), (v, vf))[kind]
        return pltpu.make_async_remote_copy(
            src_ref=src.at[:, :, columns(whole_head(device))],
            dst_ref=dst.at[span(me, held)],
            send_sem=fsend.at[kind, step],
            recv_sem=frecv.at[kind, me],
            device_id={"seq": device},
            device_id_type=MESH,
        )

    def query_copy(step, device):
        return pltpu.make_async_remote_copy(
            src_ref=q.at[device % CORES, :, columns(shared_head(device))],
            dst_ref=qs.at[me],
            send_sem=qsend.at[step],
            recv_sem=qrecv.at[me],
            device_id={"seq": device},
            device_id_type=MESH,
        )

    def shared_copy(kind, step, device):
        src, dst = ((k, ks), (v, vs))[kind]
        return pltpu.make_async_remote_copy(
            src_ref=src.at[:, :, columns(shared_head(device))],
            dst_ref=dst.at[span(me, held)],
            send_sem=csend.at[kind, step],
            recv_sem=crecv.at[kind, me],
            device_id={"seq": device},
            device_id_type=MESH,
        )

    def forward_copy(kind, step, origin):
        buf = (ks, vs)[kind]
        return pltpu.make_async_remote_copy(
            src_ref=buf.at[span(origin, held)],
            dst_ref=buf.at[span(origin, held)],
            send_sem=wsend.at[kind, step],
            recv_sem=crecv.at[kind, origin],
            device_id={"seq": sibling},
            device_id_type=MESH,
        )

    def result_copy(buf, index, slot, head, tile):
        return pltpu.make_async_remote_copy(
            src_ref=buf.at[index],
            dst_ref=out.at[:, columns(pan * heads + head)],
            send_sem=osend.at[slot],
            recv_sem=orecv.at[pan * heads + head],
            device_id={"seq": tile // panels, "panel": tile % panels},
            device_id_type=MESH,
        )

    barrier = pltpu.get_barrier_semaphore()

    def greet(step, carry):
        other = (flat + step) % (n * panels)
        pl.semaphore_signal(
            barrier, inc=1,
            device_id={"seq": other // panels, "panel": other % panels},
            device_id_type=MESH,
        )
        return carry

    lax.fori_loop(1, n * panels, greet, 0)

    own = [
        pltpu.make_async_copy(src.at[:, :, columns(whole_head(me))], dst.at[span(me, held)], frecv.at[kind, me])
        for kind, (src, dst) in enumerate(((k, kf), (q, qf), (v, vf)))
    ]
    own.append(
        pltpu.make_async_copy(
            q.at[core, :, columns(shared_head(me))], qs.at[me], qrecv.at[me]
        )
    )
    own += [
        pltpu.make_async_copy(src.at[:, :, columns(shared_head(me))], dst.at[span(me, held)], crecv.at[kind, me])
        for kind, (src, dst) in enumerate(((k, ks), (v, vs)))
    ]
    for copy in own:
        copy.start()

    pl.semaphore_wait(barrier, n * panels - 1)

    def send_full(step, carry):
        device = (me + step) % n
        for kind in range(3):
            full_copy(kind, step, device).start()
        return carry

    lax.fori_loop(1, n, send_full, 0)

    def send_shared(step, carry):
        device = ((chip + step) % chips) * CORES + core
        for kind in range(2):
            shared_copy(kind, step, device).start()
        return carry

    lax.fori_loop(1, chips, send_shared, 0)
    for kind in range(2):
        shared_copy(kind, 0, sibling).start()

    def send_query(step, carry):
        query_copy(step, (me + step) % n).start()
        return carry

    lax.fori_loop(1, n, send_query, 0)

    def attend(query, head, tile, keys, values):
        blocks = [lists[head, tile, j] for j in range(listed)]
        live = counts[head, tile]
        scores = []
        for j in range(listed):
            dots = lax.dot_general(
                query, keys[blocks[j]], (((1,), (1,)), ((), ())), preferred_element_type=jnp.float32
            )
            scores.append(dots + jnp.minimum(live - 1 - j, 0).astype(jnp.float32) * 1e30)
        top = functools.reduce(jnp.maximum, scores)
        top = jnp.max(top, axis=1, keepdims=True)
        weights = [jnp.exp((s - top) * scale) for s in scores]
        total = jnp.sum(functools.reduce(jnp.add, weights), axis=1, keepdims=True)
        mixed = functools.reduce(
            jnp.add,
            [
                jnp.dot(w.astype(jnp.bfloat16), values[blocks[j]], preferred_element_type=jnp.float32)
                for j, w in enumerate(weights)
            ],
        )
        return (mixed / total).astype(jnp.bfloat16)

    def ship(buf, index, slot, head, tile):
        home = tile == flat

        @pl.when(home)
        def _():
            pltpu.make_async_copy(
                buf.at[index], out.at[:, columns(pan * heads + head)], orecv.at[pan * heads + head]
            ).start()

        @pl.when(jnp.logical_not(home))
        def _():
            result_copy(buf, index, slot, head, tile).start()

    def wait_full(src, carry):
        for kind, (ref, dst) in enumerate(((k, kf), (q, qf), (v, vf))):
            pltpu.make_async_copy(
                ref.at[:, :, columns(0)], dst.at[span(src, held)], frecv.at[kind, src]
            ).wait()
        return carry

    lax.fori_loop(0, n, wait_full, 0)

    def full_pair(step, carry):
        device = (me + step) % n
        mine = whole_head(me)
        for place in range(panels):
            tile = device * panels + place
            of[tile] = attend(qf[tile], mine, tile, kf, vf)
            ship(of, tile, tile, mine, tile)
        return carry

    lax.fori_loop(1, n + 1, full_pair, 0)

    def wait_shared(kind, origin):
        ref, dst = ((k, ks), (v, vs))[kind]
        pltpu.make_async_copy(
            ref.at[:, :, columns(0)], dst.at[span(origin, held)], crecv.at[kind, origin]
        ).wait()

    def forward(step, carry):
        origin = ((chip + step) % chips) * CORES + core
        for kind in range(2):
            wait_shared(kind, origin)
            forward_copy(kind, step, origin).start()
        return carry

    lax.fori_loop(1, chips, forward, 0)
    for kind in range(2):
        wait_shared(kind, me)

    def wait_query(src, carry):
        pltpu.make_async_copy(
            q.at[0, :, columns(0)], qs.at[src], qrecv.at[src]
        ).wait()
        return carry

    lax.fori_loop(0, n, wait_query, 0)

    def wait_other(step, carry):
        for kind in range(2):
            wait_shared(kind, step * CORES + 1 - core)
        return carry

    lax.fori_loop(0, chips, wait_other, 0)

    def half_pair(step, carry):
        mine = shared_head(me)
        for place in range(2):
            device = (me + 1 + step * 2 + place) % n
            tile = device * panels + core
            os[device] = attend(qs[device], mine, tile, ks, vs)
            ship(os, device, tiles + device, mine, tile)
        return carry

    lax.fori_loop(0, n // 2, half_pair, 0)

    def finish_sends(step, carry):
        device = (me + step) % n
        for kind in range(3):
            full_copy(kind, step, device).wait_send()
        query_copy(step, device).wait_send()
        return carry

    lax.fori_loop(1, n, finish_sends, 0)

    def finish_shared(step, carry):
        device = ((chip + step) % chips) * CORES + core
        for kind in range(2):
            shared_copy(kind, step, device).wait_send()
            forward_copy(kind, step, device).wait_send()
        return carry

    lax.fori_loop(1, chips, finish_shared, 0)
    for kind in range(2):
        shared_copy(kind, 0, sibling).wait_send()

    def finish_full_results(step, carry):
        tile = (flat + step) % tiles
        result_copy(of, tile, tile, whole_head(me), tile).wait_send()
        return carry

    lax.fori_loop(1, tiles, finish_full_results, 0)

    def finish_half_results(device, carry):
        tile = device * panels + core

        @pl.when(tile != flat)
        def _():
            result_copy(os, device, tiles + device, shared_head(me), tile).wait_send()

        return carry

    lax.fori_loop(0, n, finish_half_results, 0)

    def receive(head, carry):
        pltpu.make_async_copy(of.at[0], out.at[:, columns(head)], orecv.at[head]).wait()
        return carry

    lax.fori_loop(0, heads * panels, receive, 0)


def spread(n, panels, queries, key_rows, value_rows, block_lists, block_counts):
    rows, width = queries.shape
    heads = width // HEAD_DIM
    trio = CORES * heads // n
    tiles = n * panels
    kind = queries.dtype
    whole = pltpu.VMEM((tiles, BLOCK, HEAD_DIM), kind)
    dma = pltpu.SemaphoreType.DMA
    chips = n // CORES
    smem = pl.BlockSpec(memory_space=pltpu.SMEM)
    anywhere = pl.BlockSpec(memory_space=pl.ANY)
    return pl.pallas_call(
        functools.partial(spread_kernel, n, panels, heads, trio),
        out_shape=jax.ShapeDtypeStruct((BLOCK, width * panels), kind),
        in_specs=[smem, smem, anywhere, anywhere, anywhere],
        out_specs=anywhere,
        scratch_shapes=[
            whole, whole, whole,
            pltpu.VMEM((n, BLOCK, HEAD_DIM), kind), whole, whole,
            pltpu.VMEM((tiles, BLOCK, HEAD_DIM), kind),
            pltpu.VMEM((n, BLOCK, HEAD_DIM), kind),
            dma((3, n)), dma((3, n)),
            dma((n,)), dma((n,)),
            dma((2, chips)), dma((2, n)), dma((2, chips)),
            dma((tiles + n,)), dma((heads * panels,)),
        ],
        compiler_params=pltpu.CompilerParams(
            collective_id=0, has_side_effects=True, vmem_limit_bytes=48 * 1024 * 1024
        ),
        name="spread_heads",
    )(block_lists, block_counts, *(x.reshape(-1, BLOCK, width) for x in (queries, key_rows, value_rows)))


def solution(mesh):
    n, panels = mesh.shape["seq"], mesh.shape["panel"]

    def shards(queries, key_rows, value_rows, block_lists, block_counts):
        rows, width = queries.shape
        heads = width // HEAD_DIM
        fits = (
            n % CORES == 0
            and panels == CORES
            and rows == panels * BLOCK
            and CORES * heads == (CORES + 1) * n
        )
        if fits:
            return spread(n, panels, queries, key_rows, value_rows, block_lists, block_counts)
        return gathered(queries, key_rows, value_rows, block_lists, block_counts)

    return jax.shard_map(
        shards,
        mesh=mesh,
        in_specs=(
            P(("groups", "seq"), "panel"),
            P(("groups", "seq"), "panel"),
            P(("groups", "seq"), "panel"),
            P("panel", None, None),
            P("panel", None),
        ),
        out_specs=P(("groups", "seq", "panel"), None),
        check_vma=False,
    )
```

```python
import functools

import jax
import jax.numpy as jnp
from jax import lax
from jax.experimental import pallas as pl
from jax.experimental.pallas import tpu as pltpu
from jax.sharding import PartitionSpec as P

HEAD_DIM = 128
BLOCK = 128
CORES = 2
MESH = pl.DeviceIdType.MESH


def gathered(queries, key_rows, value_rows, block_lists, block_counts):
    local_rows = queries.shape[0]
    heads_here = queries.shape[1] // HEAD_DIM
    tiles_here = local_rows // BLOCK
    listed_len = block_lists.shape[2]
    scale = HEAD_DIM ** (-0.5)
    position = lax.axis_index("seq")
    my_lists = lax.dynamic_slice_in_dim(block_lists, position * tiles_here, tiles_here, 1)
    my_counts = lax.dynamic_slice_in_dim(block_counts, position * tiles_here, tiles_here, 1)
    slot_live = jnp.arange(listed_len, dtype=jnp.int32)[None, None, :] < my_counts[:, :, None]
    query_heads = queries.reshape(local_rows, heads_here, HEAD_DIM).transpose(1, 0, 2)
    key_piece = lax.all_gather(key_rows, "seq", axis=0, tiled=True)
    value_piece = lax.all_gather(value_rows, "seq", axis=0, tiled=True)
    piece_rows = key_piece.shape[0]
    piece_ids = jnp.arange(piece_rows // BLOCK, dtype=jnp.int32)
    hits = (my_lists[:, :, :, None] == piece_ids[None, None, None, :]) & slot_live[:, :, :, None]
    keep = jnp.any(hits, axis=2)
    key_heads = key_piece.reshape(piece_rows, heads_here, HEAD_DIM).transpose(1, 0, 2)
    value_heads = value_piece.reshape(piece_rows, heads_here, HEAD_DIM).transpose(1, 0, 2)

    def one_head(items):
        query_head, key_head, value_head, keep_head = items
        mask = jnp.repeat(jnp.repeat(keep_head, BLOCK, axis=0), BLOCK, axis=1)
        scores = (
            lax.dot_general(
                query_head, key_head, (((1,), (1,)), ((), ())), preferred_element_type=jnp.float32
            )
            * scale
        )
        masked = jnp.where(mask, scores, -1e30)
        top = jnp.max(masked, axis=1, keepdims=True)
        weights = jnp.where(mask, jnp.exp(masked - top), 0.0)
        total = jnp.sum(weights, axis=1, keepdims=True)
        mixed = jnp.dot(weights.astype(jnp.bfloat16), value_head, preferred_element_type=jnp.float32)
        return (mixed / total).astype(jnp.bfloat16)

    results = lax.map(one_head, (query_heads, key_heads, value_heads, keep))
    joined = results.transpose(1, 0, 2).reshape(local_rows, heads_here * HEAD_DIM)
    return lax.all_to_all(joined, "panel", split_axis=0, concat_axis=1, tiled=True)


def spread_kernel(
    n, panels, heads, trio,
    lists, counts, q, k, v, out,
    qf, kf, vf, qs, ks, vs, of, os,
    fsend, frecv, qsend, qrecv, csend, crecv, wsend, osend, orecv,
):
    me = lax.axis_index("seq")
    pan = lax.axis_index("panel")
    chip, core = me // CORES, me % CORES
    chips = n // CORES
    sibling = chip * CORES + 1 - core
    held = q.shape[0]
    listed = lists.shape[1]
    tiles = n * panels
    scale = HEAD_DIM ** (-0.5)
    flat = me * panels + pan

    def columns(head):
        return pl.ds(pl.multiple_of(head * HEAD_DIM, HEAD_DIM), HEAD_DIM)

    def span(at, size):
        return pl.ds(pl.multiple_of(at * size, size), size)

    def whole_head(device):
        return (device // CORES) * trio + device % CORES

    def shared_head(device):
        return (device // CORES) * trio + CORES

    def full_copy(kind, step, device):
        src, dst = ((k, kf), (q, qf), (v, vf))[kind]
        return pltpu.make_async_remote_copy(
            src_ref=src.at[:, :, columns(whole_head(device))],
            dst_ref=dst.at[span(me, held)],
            send_sem=fsend.at[kind, step],
            recv_sem=frecv.at[kind, me],
            device_id={"seq": device},
            device_id_type=MESH,
        )

    def query_copy(step, device):
        return pltpu.make_async_remote_copy(
            src_ref=q.at[device % CORES, :, columns(shared_head(device))],
            dst_ref=qs.at[me],
            send_sem=qsend.at[step],
            recv_sem=qrecv.at[me],
            device_id={"seq": device},
            device_id_type=MESH,
        )

    def shared_copy(kind, step, device):
        src, dst = ((k, ks), (v, vs))[kind]
        return pltpu.make_async_remote_copy(
            src_ref=src.at[:, :, columns(shared_head(device))],
            dst_ref=dst.at[span(me, held)],
            send_sem=csend.at[kind, step],
            recv_sem=crecv.at[kind, me],
            device_id={"seq": device},
            device_id_type=MESH,
        )

    def forward_copy(kind, step, origin):
        buf = (ks, vs)[kind]
        return pltpu.make_async_remote_copy(
            src_ref=buf.at[span(origin, held)],
            dst_ref=buf.at[span(origin, held)],
            send_sem=wsend.at[kind, step],
            recv_sem=crecv.at[kind, origin],
            device_id={"seq": sibling},
            device_id_type=MESH,
        )

    def result_copy(buf, index, slot, head, tile):
        return pltpu.make_async_remote_copy(
            src_ref=buf.at[index],
            dst_ref=out.at[:, columns(pan * heads + head)],
            send_sem=osend.at[slot],
            recv_sem=orecv.at[pan * heads + head],
            device_id={"seq": tile // panels, "panel": tile % panels},
            device_id_type=MESH,
        )

    barrier = pltpu.get_barrier_semaphore()

    def greet(step, carry):
        other = (flat + step) % (n * panels)
        pl.semaphore_signal(
            barrier, inc=1,
            device_id={"seq": other // panels, "panel": other % panels},
            device_id_type=MESH,
        )
        return carry

    lax.fori_loop(1, n * panels, greet, 0)

    own = [
        pltpu.make_async_copy(src.at[:, :, columns(whole_head(me))], dst.at[span(me, held)], frecv.at[kind, me])
        for kind, (src, dst) in enumerate(((k, kf), (q, qf), (v, vf)))
    ]
    own.append(
        pltpu.make_async_copy(
            q.at[core, :, columns(shared_head(me))], qs.at[me], qrecv.at[me]
        )
    )
    own += [
        pltpu.make_async_copy(src.at[:, :, columns(shared_head(me))], dst.at[span(me, held)], crecv.at[kind, me])
        for kind, (src, dst) in enumerate(((k, ks), (v, vs)))
    ]
    for copy in own:
        copy.start()

    pl.semaphore_wait(barrier, n * panels - 1)

    def send_full(step, carry):
        device = (me + step) % n
        for kind in range(3):
            full_copy(kind, step, device).start()
        return carry

    lax.fori_loop(1, n, send_full, 0)

    def sent_full(step):
        for kind in range(3):
            full_copy(kind, step, (me + step) % n).wait_send()
        query_copy(step, (me + step) % n).start()

    def send_shared(step, carry):
        sent_full(CORES * step - 1)
        sent_full(CORES * step)
        device = ((chip + step) % chips) * CORES + core
        for kind in range(2):
            shared_copy(kind, step, device).start()
        return carry

    lax.fori_loop(1, chips, send_shared, 0)
    sent_full(n - 1)
    for kind in range(2):
        shared_copy(kind, 0, sibling).start()

    def attend(query, head, tile, keys, values):
        blocks = [lists[head, j, tile] for j in range(listed)]
        live = counts[head, tile]
        key_part = jnp.concatenate([keys[b] for b in blocks], axis=0)
        dots = lax.dot_general(
            query, key_part, (((1,), (1,)), ((), ())), preferred_element_type=jnp.float32
        )
        scores = [
            dots[:, j * BLOCK : (j + 1) * BLOCK] + jnp.minimum(live - 1 - j, 0).astype(jnp.float32) * 1e30
            for j in range(listed)
        ]
        top = jnp.max(functools.reduce(jnp.maximum, scores), axis=1, keepdims=True)
        weights = [jnp.exp((s - top) * scale) for s in scores]
        total = jnp.sum(functools.reduce(jnp.add, weights), axis=1, keepdims=True)
        rounded = jnp.concatenate([w.astype(jnp.bfloat16) for w in weights], axis=1)
        value_part = jnp.concatenate([values[b] for b in blocks], axis=0)
        mixed = jnp.dot(rounded, value_part, preferred_element_type=jnp.float32)
        return (mixed / total).astype(jnp.bfloat16)

    results = lax.map(one_head, (query_heads, key_heads, value_heads, keep))
    joined = results.transpose(1, 0, 2).reshape(local_rows, heads_here * HEAD_DIM)
    return lax.all_to_all(joined, "panel", split_axis=0, concat_axis=1, tiled=True)


def spread_kernel(
    n, panels, heads, trio,
    lists, counts, q, k, v, out,
    qf, kf, vf, qs, ks, vs, of, os,
    fsend, frecv, qsend, qrecv, csend, crecv, wsend, osend, orecv,
):
    me = lax.axis_index("seq")
    pan = lax.axis_index("panel")
    chip, core = me // CORES, me % CORES
    chips = n // CORES
    sibling = chip * CORES + 1 - core
    held = q.shape[0]
    listed = lists.shape[1]
    tiles = n * panels
    scale = HEAD_DIM ** (-0.5)
    flat = me * panels + pan

    def columns(head):
        return pl.ds(pl.multiple_of(head * HEAD_DIM, HEAD_DIM), HEAD_DIM)

    def span(at, size):
        return pl.ds(pl.multiple_of(at * size, size), size)

    def whole_head(device):
        return (device // CORES) * trio + device % CORES

    def shared_head(device):
        return (device // CORES) * trio + CORES

    def full_copy(kind, step, device):
        src, dst = ((k, kf), (q, qf), (v, vf))[kind]
        return pltpu.make_async_remote_copy(
            src_ref=src.at[:, :, columns(whole_head(device))],
            dst_ref=dst.at[span(me, held)],
            send_sem=fsend.at[kind, step],
            recv_sem=frecv.at[kind, me],
            device_id={"seq": device},
            device_id_type=MESH,
        )

    def query_copy(step, device):
        return pltpu.make_async_remote_copy(
            src_ref=q.at[device % CORES, :, columns(shared_head(device))],
            dst_ref=qs.at[me],
            send_sem=qsend.at[step],
            recv_sem=qrecv.at[me],
            device_id={"seq": device},
            device_id_type=MESH,
        )

    def shared_copy(kind, step, device):
        src, dst = ((k, ks), (v, vs))[kind]
        return pltpu.make_async_remote_copy(
            src_ref=src.at[:, :, columns(shared_head(device))],
            dst_ref=dst.at[span(me, held)],
            send_sem=csend.at[kind, step],
            recv_sem=crecv.at[kind, me],
            device_id={"seq": device},
            device_id_type=MESH,
        )

    def forward_copy(kind, step, origin):
        buf = (ks, vs)[kind]
        return pltpu.make_async_remote_copy(
            src_ref=buf.at[span(origin, held)],
            dst_ref=buf.at[span(origin, held)],
            send_sem=wsend.at[kind, step],
            recv_sem=crecv.at[kind, origin],
            device_id={"seq": sibling},
            device_id_type=MESH,
        )

    def result_copy(buf, index, slot, head, tile):
        return pltpu.make_async_remote_copy(
            src_ref=buf.at[index],
            dst_ref=out.at[:, columns(pan * heads + head)],
            send_sem=osend.at[slot],
            recv_sem=orecv.at[pan * heads + head],
            device_id={"seq": tile // panels, "panel": tile % panels},
            device_id_type=MESH,
        )

    barrier = pltpu.get_barrier_semaphore()

    def greet(step, carry):
        other = (flat + step) % (n * panels)
        pl.semaphore_signal(
            barrier, inc=1,
            device_id={"seq": other // panels, "panel": other % panels},
            device_id_type=MESH,
        )
        return carry

    lax.fori_loop(1, n * panels, greet, 0)

    own = [
        pltpu.make_async_copy(src.at[:, :, columns(whole_head(me))], dst.at[span(me, held)], frecv.at[kind, me])
        for kind, (src, dst) in enumerate(((k, kf), (q, qf), (v, vf)))
    ]
    own.append(
        pltpu.make_async_copy(
            q.at[core, :, columns(shared_head(me))], qs.at[me], qrecv.at[me]
        )
    )
    own += [
        pltpu.make_async_copy(src.at[:, :, columns(shared_head(me))], dst.at[span(me, held)], crecv.at[kind, me])
        for kind, (src, dst) in enumerate(((k, ks), (v, vs)))
    ]
    for copy in own:
        copy.start()

    pl.semaphore_wait(barrier, n * panels - 1)

    def send_full(step, carry):
        device = (me + step) % n
        for kind in range(3):
            full_copy(kind, step, device).start()
        return carry

    lax.fori_loop(1, n, send_full, 0)

    def sent_full(step):
        for kind in range(3):
            full_copy(kind, step, (me + step) % n).wait_send()
        query_copy(step, (me + step) % n).start()

    def send_shared(step, carry):
        sent_full(CORES * step - 1)
        sent_full(CORES * step)
        device = ((chip + step) % chips) * CORES + core
        for kind in range(2):
            shared_copy(kind, step, device).start()
        return carry

    lax.fori_loop(1, chips, send_shared, 0)
    sent_full(n - 1)
    for kind in range(2):
        shared_copy(kind, 0, sibling).start()

    def attend(query, head, tile, keys, values):
        blocks = [lists[head, j, tile] for j in range(listed)]
        live = counts[head, tile]
        scores = []
        for j in range(listed):
            dots = lax.dot_general(
                query, keys[blocks[j]], (((1,), (1,)), ((), ())), preferred_element_type=jnp.float32
            )
            scores.append(dots + jnp.minimum(live - 1 - j, 0).astype(jnp.float32) * 1e30)
        top = functools.reduce(jnp.maximum, scores)
        top = jnp.max(top, axis=1, keepdims=True)
        weights = [jnp.exp((s - top) * scale) for s in scores]
        total = jnp.sum(functools.reduce(jnp.add, weights), axis=1, keepdims=True)
        mixed = functools.reduce(
            jnp.add,
            [
                jnp.dot(w.astype(jnp.bfloat16), values[blocks[j]], preferred_element_type=jnp.float32)
                for j, w in enumerate(weights)
            ],
        )
        return (mixed / total).astype(jnp.bfloat16)

    def ship(buf, index, slot, head, tile):
        home = tile == flat

        @pl.when(home)
        def _():
            pltpu.make_async_copy(
                buf.at[index], out.at[:, columns(pan * heads + head)], orecv.at[pan * heads + head]
            ).start()

        @pl.when(jnp.logical_not(home))
        def _():
            result_copy(buf, index, slot, head, tile).start()

    def wait_full(src, carry):
        for kind, (ref, dst) in enumerate(((k, kf), (q, qf), (v, vf))):
            pltpu.make_async_copy(
                ref.at[:, :, columns(0)], dst.at[span(src, held)], frecv.at[kind, src]
            ).wait()
        return carry

    lax.fori_loop(0, n, wait_full, 0)

    def full_pair(step, carry):
        device = (me + step) % n
        mine = whole_head(me)
        for place in range(panels):
            tile = device * panels + place
            of[tile] = attend(qf[tile], mine, tile, kf, vf)
            ship(of, tile, tile, mine, tile)
        return carry

    lax.fori_loop(1, n + 1, full_pair, 0)

    def wait_shared(kind, origin):
        ref, dst = ((k, ks), (v, vs))[kind]
        pltpu.make_async_copy(
            ref.at[:, :, columns(0)], dst.at[span(origin, held)], crecv.at[kind, origin]
        ).wait()

    def forward(step, carry):
        origin = ((chip + step) % chips) * CORES + core
        for kind in range(2):
            wait_shared(kind, origin)
            forward_copy(kind, step, origin).start()
        return carry

    lax.fori_loop(1, chips, forward, 0)
    for kind in range(2):
        wait_shared(kind, me)

    def wait_query(src, carry):
        pltpu.make_async_copy(
            q.at[0, :, columns(0)], qs.at[src], qrecv.at[src]
        ).wait()
        return carry

    lax.fori_loop(0, n, wait_query, 0)

    def wait_other(step, carry):
        for kind in range(2):
            wait_shared(kind, step * CORES + 1 - core)
        return carry

    lax.fori_loop(0, chips, wait_other, 0)

    def half_pair(step, carry):
        mine = shared_head(me)
        for place in range(2):
            device = (me + 1 + step * 2 + place) % n
            tile = device * panels + core
            os[device] = attend(qs[device], mine, tile, ks, vs)
            ship(os, device, tiles + device, mine, tile)
        return carry

    lax.fori_loop(0, n // 2, half_pair, 0)

    def finish_sends(step, carry):
        device = (me + step) % n
        query_copy(step, device).wait_send()
        return carry

    lax.fori_loop(1, n, finish_sends, 0)

    def finish_shared(step, carry):
        device = ((chip + step) % chips) * CORES + core
        for kind in range(2):
            shared_copy(kind, step, device).wait_send()
            forward_copy(kind, step, device).wait_send()
        return carry

    lax.fori_loop(1, chips, finish_shared, 0)
    for kind in range(2):
        shared_copy(kind, 0, sibling).wait_send()

    def finish_full_results(step, carry):
        tile = (flat + step) % tiles
        result_copy(of, tile, tile, whole_head(me), tile).wait_send()
        return carry

    lax.fori_loop(1, tiles, finish_full_results, 0)

    def finish_half_results(device, carry):
        tile = device * panels + core

        @pl.when(tile != flat)
        def _():
            result_copy(os, device, tiles + device, shared_head(me), tile).wait_send()

        return carry

    lax.fori_loop(0, n, finish_half_results, 0)

    def receive(head, carry):
        pltpu.make_async_copy(of.at[0], out.at[:, columns(head)], orecv.at[head]).wait()
        return carry

    lax.fori_loop(0, heads * panels, receive, 0)


def spread(n, panels, queries, key_rows, value_rows, block_lists, block_counts):
    rows, width = queries.shape
    heads = width // HEAD_DIM
    trio = CORES * heads // n
    tiles = n * panels
    kind = queries.dtype
    whole = pltpu.VMEM((tiles, BLOCK, HEAD_DIM), kind)
    dma = pltpu.SemaphoreType.DMA
    chips = n // CORES
    smem = pl.BlockSpec(memory_space=pltpu.SMEM)
    anywhere = pl.BlockSpec(memory_space=pl.ANY)
    return pl.pallas_call(
        functools.partial(spread_kernel, n, panels, heads, trio),
        out_shape=jax.ShapeDtypeStruct((BLOCK, width * panels), kind),
        in_specs=[smem, smem, anywhere, anywhere, anywhere],
        out_specs=anywhere,
        scratch_shapes=[
            whole, whole, whole,
            pltpu.VMEM((n, BLOCK, HEAD_DIM), kind), whole, whole,
            pltpu.VMEM((tiles, BLOCK, HEAD_DIM), kind),
            pltpu.VMEM((n, BLOCK, HEAD_DIM), kind),
            dma((3, n)), dma((3, n)),
            dma((n,)), dma((n,)),
            dma((2, chips)), dma((2, n)), dma((2, chips)),
            dma((tiles + n,)), dma((heads * panels,)),
        ],
        compiler_params=pltpu.CompilerParams(
            collective_id=0, has_side_effects=True, vmem_limit_bytes=62 * 1024 * 1024
        ),
        name="spread_heads",
    )(block_lists.transpose(0, 2, 1), block_counts, *(x.reshape(-1, BLOCK, width) for x in (queries, key_rows, value_rows)))


def solution(mesh):
    n, panels = mesh.shape["seq"], mesh.shape["panel"]

    def shards(queries, key_rows, value_rows, block_lists, block_counts):
        rows, width = queries.shape
        heads = width // HEAD_DIM
        fits = (
            n % CORES == 0
            and panels == CORES
            and rows == panels * BLOCK
            and CORES * heads == (CORES + 1) * n
        )
        if fits:
            return spread(n, panels, queries, key_rows, value_rows, block_lists, block_counts)
        return gathered(queries, key_rows, value_rows, block_lists, block_counts)

    return jax.shard_map(
        shards,
        mesh=mesh,
        in_specs=(
            P(("groups", "seq"), "panel"),
            P(("groups", "seq"), "panel"),
            P(("groups", "seq"), "panel"),
            P("panel", None, None),
            P("panel", None),
        ),
        out_specs=P(("groups", "seq", "panel"), None),
        check_vma=False,
    )
```

```python
import functools

import jax
import jax.numpy as jnp
from jax import lax
from jax.experimental import pallas as pl
from jax.experimental.pallas import tpu as pltpu
from jax.sharding import PartitionSpec as P

HEAD_DIM = 128
BLOCK = 128
CORES = 2
MESH = pl.DeviceIdType.MESH


def gathered(queries, key_rows, value_rows, block_lists, block_counts):
    local_rows = queries.shape[0]
    heads_here = queries.shape[1] // HEAD_DIM
    tiles_here = local_rows // BLOCK
    listed_len = block_lists.shape[2]
    scale = HEAD_DIM ** (-0.5)
    position = lax.axis_index("seq")
    my_lists = lax.dynamic_slice_in_dim(block_lists, position * tiles_here, tiles_here, 1)
    my_counts = lax.dynamic_slice_in_dim(block_counts, position * tiles_here, tiles_here, 1)
    slot_live = jnp.arange(listed_len, dtype=jnp.int32)[None, None, :] < my_counts[:, :, None]
    query_heads = queries.reshape(local_rows, heads_here, HEAD_DIM).transpose(1, 0, 2)
    key_piece = lax.all_gather(key_rows, "seq", axis=0, tiled=True)
    value_piece = lax.all_gather(value_rows, "seq", axis=0, tiled=True)
    piece_rows = key_piece.shape[0]
    piece_ids = jnp.arange(piece_rows // BLOCK, dtype=jnp.int32)
    hits = (my_lists[:, :, :, None] == piece_ids[None, None, None, :]) & slot_live[:, :, :, None]
    keep = jnp.any(hits, axis=2)
    key_heads = key_piece.reshape(piece_rows, heads_here, HEAD_DIM).transpose(1, 0, 2)
    value_heads = value_piece.reshape(piece_rows, heads_here, HEAD_DIM).transpose(1, 0, 2)

    def one_head(items):
        query_head, key_head, value_head, keep_head = items
        mask = jnp.repeat(jnp.repeat(keep_head, BLOCK, axis=0), BLOCK, axis=1)
        scores = (
            lax.dot_general(
                query_head, key_head, (((1,), (1,)), ((), ())), preferred_element_type=jnp.float32
            )
            * scale
        )
        masked = jnp.where(mask, scores, -1e30)
        top = jnp.max(masked, axis=1, keepdims=True)
        weights = jnp.where(mask, jnp.exp(masked - top), 0.0)
        total = jnp.sum(weights, axis=1, keepdims=True)
        mixed = jnp.dot(weights.astype(jnp.bfloat16), value_head, preferred_element_type=jnp.float32)
        return (mixed / total).astype(jnp.bfloat16)

    results = lax.map(one_head, (query_heads, key_heads, value_heads, keep))
    joined = results.transpose(1, 0, 2).reshape(local_rows, heads_here * HEAD_DIM)
    return lax.all_to_all(joined, "panel", split_axis=0, concat_axis=1, tiled=True)


def spread_kernel(
    n, panels, heads, trio,
    lists, counts, q, k, v, out,
    qf, kf, vf, qs, ks, vs, of, os,
    fsend, frecv, qsend, qrecv, csend, crecv, wsend, osend, orecv,
):
    me = lax.axis_index("seq")
    pan = lax.axis_index("panel")
    chip, core = me // CORES, me % CORES
    chips = n // CORES
    sibling = chip * CORES + 1 - core
    held = q.shape[0]
    listed = lists.shape[1]
    tiles = n * panels
    scale = HEAD_DIM ** (-0.5)
    flat = me * panels + pan

    half, side = n // 2, me // (n // 2)

    def peer(step):
        far = (1 - side) * half + (me + step) % half
        near = side * half + (me + step + 1) % half
        return jnp.where(step < half, far, near)

    def peer_or_me(step):
        return jnp.where(step == n - 1, me, peer(step))

    def chip_peer(step):
        many = chips // 2
        where = chip // many
        far = (1 - where) * many + (chip + step) % many
        near = where * many + (chip + step + 1) % many
        return jnp.where(step < many, far, near) * CORES + core

    def columns(head):
        return pl.ds(pl.multiple_of(head * HEAD_DIM, HEAD_DIM), HEAD_DIM)

    def span(at, size):
        return pl.ds(pl.multiple_of(at * size, size), size)

    def whole_head(device):
        return (device // CORES) * trio + device % CORES

    def shared_head(device):
        return (device // CORES) * trio + CORES

    def full_copy(kind, step, device):
        src, dst = ((k, kf), (q, qf), (v, vf))[kind]
        return pltpu.make_async_remote_copy(
            src_ref=src.at[:, :, columns(whole_head(device))],
            dst_ref=dst.at[span(me, held)],
            send_sem=fsend.at[kind, step],
            recv_sem=frecv.at[kind, me],
            device_id={"seq": device},
            device_id_type=MESH,
        )

    def query_copy(step, device):
        return pltpu.make_async_remote_copy(
            src_ref=q.at[device % CORES, :, columns(shared_head(device))],
            dst_ref=qs.at[me],
            send_sem=qsend.at[step],
            recv_sem=qrecv.at[me],
            device_id={"seq": device},
            device_id_type=MESH,
        )

    def shared_copy(kind, step, device):
        src, dst = ((k, ks), (v, vs))[kind]
        return pltpu.make_async_remote_copy(
            src_ref=src.at[:, :, columns(shared_head(device))],
            dst_ref=dst.at[span(me, held)],
            send_sem=csend.at[kind, step],
            recv_sem=crecv.at[kind, me],
            device_id={"seq": device},
            device_id_type=MESH,
        )

    def forward_copy(kind, step, origin):
        buf = (ks, vs)[kind]
        return pltpu.make_async_remote_copy(
            src_ref=buf.at[span(origin, held)],
            dst_ref=buf.at[span(origin, held)],
            send_sem=wsend.at[kind, step],
            recv_sem=crecv.at[kind, origin],
            device_id={"seq": sibling},
            device_id_type=MESH,
        )

    def result_copy(buf, index, slot, head, tile):
        return pltpu.make_async_remote_copy(
            src_ref=buf.at[index],
            dst_ref=out.at[:, columns(pan * heads + head)],
            send_sem=osend.at[slot],
            recv_sem=orecv.at[pan * heads + head],
            device_id={"seq": tile // panels, "panel": tile % panels},
            device_id_type=MESH,
        )

    barrier = pltpu.get_barrier_semaphore()

    def greet(step, carry):
        other = (flat + step) % (n * panels)
        pl.semaphore_signal(
            barrier, inc=1,
            device_id={"seq": other // panels, "panel": other % panels},
            device_id_type=MESH,
        )
        return carry

    lax.fori_loop(1, n * panels, greet, 0)

    own = [
        pltpu.make_async_copy(src.at[:, :, columns(whole_head(me))], dst.at[span(me, held)], frecv.at[kind, me])
        for kind, (src, dst) in enumerate(((k, kf), (q, qf), (v, vf)))
    ]
    own.append(
        pltpu.make_async_copy(
            q.at[core, :, columns(shared_head(me))], qs.at[me], qrecv.at[me]
        )
    )
    own += [
        pltpu.make_async_copy(src.at[:, :, columns(shared_head(me))], dst.at[span(me, held)], crecv.at[kind, me])
        for kind, (src, dst) in enumerate(((k, ks), (v, vs)))
    ]
    for copy in own:
        copy.start()

    pl.semaphore_wait(barrier, n * panels - 1)

    def send_full(step, carry):
        for kind in range(3):
            full_copy(kind, step, peer(step)).start()
        return carry

    lax.fori_loop(0, n - 1, send_full, 0)

    def send_shared(step, carry):
        for kind in range(2):
            shared_copy(kind, step, chip_peer(step)).start()
        return carry

    lax.fori_loop(0, chips - 1, send_shared, 0)
    for kind in range(2):
        shared_copy(kind, chips - 1, sibling).start()

    def send_query(step, carry):
        query_copy(step, peer(step)).start()
        return carry

    lax.fori_loop(0, n - 1, send_query, 0)

    def attend(query, head, tile, keys, values):
        blocks = [lists[head, j, tile] for j in range(listed)]
        live = counts[head, tile]
        key_part = jnp.concatenate([keys[b] for b in blocks], axis=0)
        dots = lax.dot_general(
            query, key_part, (((1,), (1,)), ((), ())), preferred_element_type=jnp.float32
        )
        scores = [
            dots[:, j * BLOCK : (j + 1) * BLOCK] + jnp.minimum(live - 1 - j, 0).astype(jnp.float32) * 1e30
            for j in range(listed)
        ]
        top = jnp.max(functools.reduce(jnp.maximum, scores), axis=1, keepdims=True)
        weights = [jnp.exp((s - top) * scale) for s in scores]
        total = jnp.sum(functools.reduce(jnp.add, weights), axis=1, keepdims=True)
        rounded = jnp.concatenate([w.astype(jnp.bfloat16) for w in weights], axis=1)
        value_part = jnp.concatenate([values[b] for b in blocks], axis=0)
        mixed = jnp.dot(rounded, value_part, preferred_element_type=jnp.float32)
        return (mixed / total).astype(jnp.bfloat16)

    def ship(buf, index, slot, head, tile):
        home = tile == flat

        @pl.when(home)
        def _():
            pltpu.make_async_copy(
                buf.at[index], out.at[:, columns(pan * heads + head)], orecv.at[pan * heads + head]
            ).start()

        @pl.when(jnp.logical_not(home))
        def _():
            result_copy(buf, index, slot, head, tile).start()

    def wait_full(src, carry):
        for kind, (ref, dst) in enumerate(((k, kf), (q, qf), (v, vf))):
            pltpu.make_async_copy(
                ref.at[:, :, columns(0)], dst.at[span(src, held)], frecv.at[kind, src]
            ).wait()
        return carry

    lax.fori_loop(0, n, wait_full, 0)

    def full_pair(step, carry):
        device = peer_or_me(step)
        mine = whole_head(me)
        for place in range(panels):
            tile = device * panels + place
            of[tile] = attend(qf[tile], mine, tile, kf, vf)
            ship(of, tile, tile, mine, tile)
        return carry

    lax.fori_loop(0, n, full_pair, 0)

    def wait_shared(kind, origin):
        ref, dst = ((k, ks), (v, vs))[kind]
        pltpu.make_async_copy(
            ref.at[:, :, columns(0)], dst.at[span(origin, held)], crecv.at[kind, origin]
        ).wait()

    def forward(step, carry):
        origin = chip_peer(chips - 2 - step)
        for kind in range(2):
            wait_shared(kind, origin)
            forward_copy(kind, chips - 2 - step, origin).start()
        return carry

    lax.fori_loop(0, chips - 1, forward, 0)
    for kind in range(2):
        wait_shared(kind, me)

    def wait_query(src, carry):
        pltpu.make_async_copy(
            q.at[0, :, columns(0)], qs.at[src], qrecv.at[src]
        ).wait()
        return carry

    lax.fori_loop(0, n, wait_query, 0)

    def wait_other(step, carry):
        for kind in range(2):
            wait_shared(kind, step * CORES + 1 - core)
        return carry

    lax.fori_loop(0, chips, wait_other, 0)

    def half_pair(step, carry):
        mine = shared_head(me)
        for place in range(2):
            device = peer_or_me(step * 2 + place)
            tile = device * panels + core
            os[device] = attend(qs[device], mine, tile, ks, vs)
            ship(os, device, tiles + device, mine, tile)
        return carry

    lax.fori_loop(0, n // 2, half_pair, 0)

    def finish_sends(step, carry):
        for kind in range(3):
            full_copy(kind, step, peer(step)).wait_send()
        query_copy(step, peer(step)).wait_send()
        return carry

    lax.fori_loop(0, n - 1, finish_sends, 0)

    def finish_shared(step, carry):
        for kind in range(2):
            shared_copy(kind, step, chip_peer(step)).wait_send()
            forward_copy(kind, step, chip_peer(step)).wait_send()
        return carry

    lax.fori_loop(0, chips - 1, finish_shared, 0)
    for kind in range(2):
        shared_copy(kind, chips - 1, sibling).wait_send()

    def finish_full_results(step, carry):
        tile = (flat + step) % tiles
        result_copy(of, tile, tile, whole_head(me), tile).wait_send()
        return carry

    lax.fori_loop(1, tiles, finish_full_results, 0)

    def finish_half_results(device, carry):
        tile = device * panels + core

        @pl.when(tile != flat)
        def _():
            result_copy(os, device, tiles + device, shared_head(me), tile).wait_send()

        return carry

    lax.fori_loop(0, n, finish_half_results, 0)

    def receive(head, carry):
        pltpu.make_async_copy(of.at[0], out.at[:, columns(head)], orecv.at[head]).wait()
        return carry

    lax.fori_loop(0, heads * panels, receive, 0)


def spread(n, panels, queries, key_rows, value_rows, block_lists, block_counts):
    rows, width = queries.shape
    heads = width // HEAD_DIM
    trio = CORES * heads // n
    tiles = n * panels
    kind = queries.dtype
    whole = pltpu.VMEM((tiles, BLOCK, HEAD_DIM), kind)
    dma = pltpu.SemaphoreType.DMA
    chips = n // CORES
    smem = pl.BlockSpec(memory_space=pltpu.SMEM)
    anywhere = pl.BlockSpec(memory_space=pl.ANY)
    return pl.pallas_call(
        functools.partial(spread_kernel, n, panels, heads, trio),
        out_shape=jax.ShapeDtypeStruct((BLOCK, width * panels), kind),
        in_specs=[smem, smem, anywhere, anywhere, anywhere],
        out_specs=pl.BlockSpec(memory_space=pltpu.VMEM),
        scratch_shapes=[
            whole, whole, whole,
            pltpu.VMEM((n, BLOCK, HEAD_DIM), kind), whole, whole,
            pltpu.VMEM((tiles, BLOCK, HEAD_DIM), kind),
            pltpu.VMEM((n, BLOCK, HEAD_DIM), kind),
            dma((3, n)), dma((3, n)),
            dma((n,)), dma((n,)),
            dma((2, chips)), dma((2, n)), dma((2, chips)),
            dma((tiles + n,)), dma((heads * panels,)),
        ],
        compiler_params=pltpu.CompilerParams(
            collective_id=0, has_side_effects=True, vmem_limit_bytes=62 * 1024 * 1024
        ),
        name="spread_heads",
    )(block_lists.transpose(0, 2, 1), block_counts, *(x.reshape(-1, BLOCK, width) for x in (queries, key_rows, value_rows)))


def solution(mesh):
    n, panels = mesh.shape["seq"], mesh.shape["panel"]

    def shards(queries, key_rows, value_rows, block_lists, block_counts):
        rows, width = queries.shape
        heads = width // HEAD_DIM
        fits = (
            n % (2 * CORES) == 0
            and panels == CORES
            and rows == panels * BLOCK
            and CORES * heads == (CORES + 1) * n
        )
        if fits:
            return spread(n, panels, queries, key_rows, value_rows, block_lists, block_counts)
        return gathered(queries, key_rows, value_rows, block_lists, block_counts)

    return jax.shard_map(
        shards,
        mesh=mesh,
        in_specs=(
            P(("groups", "seq"), "panel"),
            P(("groups", "seq"), "panel"),
            P(("groups", "seq"), "panel"),
            P("panel", None, None),
            P("panel", None),
        ),
        out_specs=P(("groups", "seq", "panel"), None),
        check_vma=False,
    )
```

```python
import functools

import jax
import jax.numpy as jnp
from jax import lax
from jax.experimental import pallas as pl
from jax.experimental.pallas import tpu as pltpu
from jax.sharding import PartitionSpec as P

HEAD_DIM = 128
BLOCK = 128
CORES = 2
MESH = pl.DeviceIdType.MESH


def gathered(queries, key_rows, value_rows, block_lists, block_counts):
    local_rows = queries.shape[0]
    heads_here = queries.shape[1] // HEAD_DIM
    tiles_here = local_rows // BLOCK
    listed_len = block_lists.shape[2]
    scale = HEAD_DIM ** (-0.5)
    position = lax.axis_index("seq")
    my_lists = lax.dynamic_slice_in_dim(block_lists, position * tiles_here, tiles_here, 1)
    my_counts = lax.dynamic_slice_in_dim(block_counts, position * tiles_here, tiles_here, 1)
    slot_live = jnp.arange(listed_len, dtype=jnp.int32)[None, None, :] < my_counts[:, :, None]
    query_heads = queries.reshape(local_rows, heads_here, HEAD_DIM).transpose(1, 0, 2)
    key_piece = lax.all_gather(key_rows, "seq", axis=0, tiled=True)
    value_piece = lax.all_gather(value_rows, "seq", axis=0, tiled=True)
    piece_rows = key_piece.shape[0]
    piece_ids = jnp.arange(piece_rows // BLOCK, dtype=jnp.int32)
    hits = (my_lists[:, :, :, None] == piece_ids[None, None, None, :]) & slot_live[:, :, :, None]
    keep = jnp.any(hits, axis=2)
    key_heads = key_piece.reshape(piece_rows, heads_here, HEAD_DIM).transpose(1, 0, 2)
    value_heads = value_piece.reshape(piece_rows, heads_here, HEAD_DIM).transpose(1, 0, 2)

    def one_head(items):
        query_head, key_head, value_head, keep_head = items
        mask = jnp.repeat(jnp.repeat(keep_head, BLOCK, axis=0), BLOCK, axis=1)
        scores = (
            lax.dot_general(
                query_head, key_head, (((1,), (1,)), ((), ())), preferred_element_type=jnp.float32
            )
            * scale
        )
        masked = jnp.where(mask, scores, -1e30)
        top = jnp.max(masked, axis=1, keepdims=True)
        weights = jnp.where(mask, jnp.exp(masked - top), 0.0)
        total = jnp.sum(weights, axis=1, keepdims=True)
        mixed = jnp.dot(weights.astype(jnp.bfloat16), value_head, preferred_element_type=jnp.float32)
        return (mixed / total).astype(jnp.bfloat16)

    results = lax.map(one_head, (query_heads, key_heads, value_heads, keep))
    joined = results.transpose(1, 0, 2).reshape(local_rows, heads_here * HEAD_DIM)
    return lax.all_to_all(joined, "panel", split_axis=0, concat_axis=1, tiled=True)


def spread_kernel(
    n, panels, heads, trio,
    lists, counts, q, k, v, out, sq, sk, sv,
    qf, kf, vf, qs, ks, vs, of, os,
    staged, fsend, frecv, qsend, qrecv, csend, crecv, wsend, osend, orecv,
):
    me = lax.axis_index("seq")
    pan = lax.axis_index("panel")
    chip, core = me // CORES, me % CORES
    chips = n // CORES
    sibling = chip * CORES + 1 - core
    held = q.shape[0]
    listed = lists.shape[1]
    tiles = n * panels
    scale = HEAD_DIM ** (-0.5)
    flat = me * panels + pan

    half, side = n // 2, me // (n // 2)

    def peer(step):
        far = (1 - side) * half + (me + step) % half
        near = side * half + (me + step + 1) % half
        return jnp.where(step < half, far, near)

    def peer_or_me(step):
        return jnp.where(step == n - 1, me, peer(step))

    def chip_peer(step):
        many = chips // 2
        where = chip // many
        far = (1 - where) * many + (chip + step) % many
        near = where * many + (chip + step + 1) % many
        return jnp.where(step < many, far, near) * CORES + core

    def columns(head):
        return pl.ds(pl.multiple_of(head * HEAD_DIM, HEAD_DIM), HEAD_DIM)

    def span(at, size):
        return pl.ds(pl.multiple_of(at * size, size), size)

    def whole_head(device):
        return (device // CORES) * trio + device % CORES

    def shared_head(device):
        return (device // CORES) * trio + CORES

    def full_copy(kind, step, device):
        src, dst = ((sk, kf), (sq, qf), (sv, vf))[kind]
        return pltpu.make_async_remote_copy(
            src_ref=src.at[whole_head(device)],
            dst_ref=dst.at[span(me, held)],
            send_sem=fsend.at[kind, step],
            recv_sem=frecv.at[kind, me],
            device_id={"seq": device},
            device_id_type=MESH,
        )

    def query_copy(step, device):
        return pltpu.make_async_remote_copy(
            src_ref=sq.at[shared_head(device), device % CORES],
            dst_ref=qs.at[me],
            send_sem=qsend.at[step],
            recv_sem=qrecv.at[me],
            device_id={"seq": device},
            device_id_type=MESH,
        )

    def shared_copy(kind, step, device):
        src, dst = ((sk, ks), (sv, vs))[kind]
        return pltpu.make_async_remote_copy(
            src_ref=src.at[shared_head(device)],
            dst_ref=dst.at[span(me, held)],
            send_sem=csend.at[kind, step],
            recv_sem=crecv.at[kind, me],
            device_id={"seq": device},
            device_id_type=MESH,
        )

    def forward_copy(kind, step, origin):
        buf = (ks, vs)[kind]
        return pltpu.make_async_remote_copy(
            src_ref=buf.at[span(origin, held)],
            dst_ref=buf.at[span(origin, held)],
            send_sem=wsend.at[kind, step],
            recv_sem=crecv.at[kind, origin],
            device_id={"seq": sibling},
            device_id_type=MESH,
        )

    def result_copy(buf, index, slot, head, tile):
        return pltpu.make_async_remote_copy(
            src_ref=buf.at[index],
            dst_ref=out.at[:, columns(pan * heads + head)],
            send_sem=osend.at[slot],
            recv_sem=orecv.at[pan * heads + head],
            device_id={"seq": tile // panels, "panel": tile % panels},
            device_id_type=MESH,
        )

    barrier = pltpu.get_barrier_semaphore()

    def greet(step, carry):
        other = (flat + step) % (n * panels)
        pl.semaphore_signal(
            barrier, inc=1,
            device_id={"seq": other // panels, "panel": other % panels},
            device_id_type=MESH,
        )
        return carry

    lax.fori_loop(1, n * panels, greet, 0)

    own = [
        pltpu.make_async_copy(src.at[:, :, columns(whole_head(me))], dst.at[span(me, held)], frecv.at[kind, me])
        for kind, (src, dst) in enumerate(((k, kf), (q, qf), (v, vf)))
    ]
    own.append(
        pltpu.make_async_copy(
            q.at[core, :, columns(shared_head(me))], qs.at[me], qrecv.at[me]
        )
    )
    own += [
        pltpu.make_async_copy(src.at[:, :, columns(shared_head(me))], dst.at[span(me, held)], crecv.at[kind, me])
        for kind, (src, dst) in enumerate(((k, ks), (v, vs)))
    ]
    def stage(kind, head):
        src, dst = ((k, sk), (q, sq), (v, sv))[kind]
        return pltpu.make_async_copy(src.at[:, :, columns(head)], dst.at[head], staged.at[kind, head])

    def start_stage(head, carry):
        for kind in range(3):
            stage(kind, head).start()
        return carry

    def wait_stage(head, carry):
        for kind in range(3):
            stage(kind, head).wait()
        return carry

    lax.fori_loop(0, heads, start_stage, 0)
    pl.semaphore_wait(barrier, n * panels - 1)
    lax.fori_loop(0, heads, wait_stage, 0)
    for copy in own:
        copy.start()

    def send_full(step, carry):
        for kind in range(3):
            full_copy(kind, step, peer(step)).start()
        return carry

    lax.fori_loop(0, n - 1, send_full, 0)

    def send_shared(step, carry):
        for kind in range(2):
            shared_copy(kind, step, chip_peer(step)).start()
        return carry

    lax.fori_loop(0, chips - 1, send_shared, 0)
    for kind in range(2):
        shared_copy(kind, chips - 1, sibling).start()

    def send_query(step, carry):
        query_copy(step, peer(step)).start()
        return carry

    lax.fori_loop(0, n - 1, send_query, 0)

    def attend(query, head, tile, keys, values):
        blocks = [lists[head, j, tile] for j in range(listed)]
        live = counts[head, tile]
        key_part = jnp.concatenate([keys[b] for b in blocks], axis=0)
        dots = lax.dot_general(
            query, key_part, (((1,), (1,)), ((), ())), preferred_element_type=jnp.float32
        )
        scores = [
            dots[:, j * BLOCK : (j + 1) * BLOCK] + jnp.minimum(live - 1 - j, 0).astype(jnp.float32) * 1e30
            for j in range(listed)
        ]
        top = jnp.max(functools.reduce(jnp.maximum, scores), axis=1, keepdims=True)
        weights = [jnp.exp((s - top) * scale) for s in scores]
        total = jnp.sum(functools.reduce(jnp.add, weights), axis=1, keepdims=True)
        rounded = jnp.concatenate([w.astype(jnp.bfloat16) for w in weights], axis=1)
        value_part = jnp.concatenate([values[b] for b in blocks], axis=0)
        mixed = jnp.dot(rounded, value_part, preferred_element_type=jnp.float32)
        return (mixed / total).astype(jnp.bfloat16)

    def ship(buf, index, slot, head, tile):
        home = tile == flat

        @pl.when(home)
        def _():
            pltpu.make_async_copy(
                buf.at[index], out.at[:, columns(pan * heads + head)], orecv.at[pan * heads + head]
            ).start()

        @pl.when(jnp.logical_not(home))
        def _():
            result_copy(buf, index, slot, head, tile).start()

    def wait_full(src, carry):
        for kind, (ref, dst) in enumerate(((k, kf), (q, qf), (v, vf))):
            pltpu.make_async_copy(
                ref.at[:, :, columns(0)], dst.at[span(src, held)], frecv.at[kind, src]
            ).wait()
        return carry

    lax.fori_loop(0, n, wait_full, 0)

    def full_pair(step, carry):
        device = peer_or_me(step)
        mine = whole_head(me)
        for place in range(panels):
            tile = device * panels + place
            of[tile] = attend(qf[tile], mine, tile, kf, vf)
            ship(of, tile, tile, mine, tile)
        return carry

    lax.fori_loop(0, n, full_pair, 0)

    def wait_shared(kind, origin):
        ref, dst = ((k, ks), (v, vs))[kind]
        pltpu.make_async_copy(
            ref.at[:, :, columns(0)], dst.at[span(origin, held)], crecv.at[kind, origin]
        ).wait()

    def forward(step, carry):
        origin = chip_peer(chips - 2 - step)
        for kind in range(2):
            wait_shared(kind, origin)
            forward_copy(kind, chips - 2 - step, origin).start()
        return carry

    lax.fori_loop(0, chips - 1, forward, 0)
    for kind in range(2):
        wait_shared(kind, me)

    def wait_query(src, carry):
        pltpu.make_async_copy(
            q.at[0, :, columns(0)], qs.at[src], qrecv.at[src]
        ).wait()
        return carry

    lax.fori_loop(0, n, wait_query, 0)

    def wait_other(step, carry):
        for kind in range(2):
            wait_shared(kind, step * CORES + 1 - core)
        return carry

    lax.fori_loop(0, chips, wait_other, 0)

    def half_pair(step, carry):
        mine = shared_head(me)
        for place in range(2):
            device = peer_or_me(step * 2 + place)
            tile = device * panels + core
            os[device] = attend(qs[device], mine, tile, ks, vs)
            ship(os, device, tiles + device, mine, tile)
        return carry

    lax.fori_loop(0, n // 2, half_pair, 0)

    def finish_sends(step, carry):
        for kind in range(3):
            full_copy(kind, step, peer(step)).wait_send()
        query_copy(step, peer(step)).wait_send()
        return carry

    lax.fori_loop(0, n - 1, finish_sends, 0)

    def finish_shared(step, carry):
        for kind in range(2):
            shared_copy(kind, step, chip_peer(step)).wait_send()
            forward_copy(kind, step, chip_peer(step)).wait_send()
        return carry

    lax.fori_loop(0, chips - 1, finish_shared, 0)
    for kind in range(2):
        shared_copy(kind, chips - 1, sibling).wait_send()

    def finish_full_results(step, carry):
        tile = (flat + step) % tiles
        result_copy(of, tile, tile, whole_head(me), tile).wait_send()
        return carry

    lax.fori_loop(1, tiles, finish_full_results, 0)

    def finish_half_results(device, carry):
        tile = device * panels + core

        @pl.when(tile != flat)
        def _():
            result_copy(os, device, tiles + device, shared_head(me), tile).wait_send()

        return carry

    lax.fori_loop(0, n, finish_half_results, 0)

    def receive(head, carry):
        pltpu.make_async_copy(of.at[0], out.at[:, columns(head)], orecv.at[head]).wait()
        return carry

    lax.fori_loop(0, heads * panels, receive, 0)


def spread(n, panels, queries, key_rows, value_rows, block_lists, block_counts):
    rows, width = queries.shape
    heads = width // HEAD_DIM
    trio = CORES * heads // n
    tiles = n * panels
    kind = queries.dtype
    whole = pltpu.VMEM((tiles, BLOCK, HEAD_DIM), kind)
    dma = pltpu.SemaphoreType.DMA
    chips = n // CORES
    smem = pl.BlockSpec(memory_space=pltpu.SMEM)
    anywhere = pl.BlockSpec(memory_space=pl.ANY)
    piled = pltpu.VMEM((heads, rows // BLOCK, BLOCK, HEAD_DIM), kind)
    return pl.pallas_call(
        functools.partial(spread_kernel, n, panels, heads, trio),
        out_shape=jax.ShapeDtypeStruct((BLOCK, width * panels), kind),
        in_specs=[smem, smem, anywhere, anywhere, anywhere],
        out_specs=anywhere,
        scratch_shapes=[
            piled, piled, piled,
            whole, whole, whole,
            pltpu.VMEM((n, BLOCK, HEAD_DIM), kind), whole, whole,
            pltpu.VMEM((tiles, BLOCK, HEAD_DIM), kind),
            pltpu.VMEM((n, BLOCK, HEAD_DIM), kind),
            dma((3, heads)), dma((3, n)), dma((3, n)),
            dma((n,)), dma((n,)),
            dma((2, chips)), dma((2, n)), dma((2, chips)),
            dma((tiles + n,)), dma((heads * panels,)),
        ],
        compiler_params=pltpu.CompilerParams(
            collective_id=0, has_side_effects=True, vmem_limit_bytes=62 * 1024 * 1024
        ),
        name="spread_heads",
    )(block_lists.transpose(0, 2, 1), block_counts, *(x.reshape(-1, BLOCK, width) for x in (queries, key_rows, value_rows)))


def solution(mesh):
    n, panels = mesh.shape["seq"], mesh.shape["panel"]

    def shards(queries, key_rows, value_rows, block_lists, block_counts):
        rows, width = queries.shape
        heads = width // HEAD_DIM
        fits = (
            n % (2 * CORES) == 0
            and panels == CORES
            and rows == panels * BLOCK
            and CORES * heads == (CORES + 1) * n
        )
        if fits:
            return spread(n, panels, queries, key_rows, value_rows, block_lists, block_counts)
        return gathered(queries, key_rows, value_rows, block_lists, block_counts)

    return jax.shard_map(
        shards,
        mesh=mesh,
        in_specs=(
            P(("groups", "seq"), "panel"),
            P(("groups", "seq"), "panel"),
            P(("groups", "seq"), "panel"),
            P("panel", None, None),
            P("panel", None),
        ),
        out_specs=P(("groups", "seq", "panel"), None),
        check_vma=False,
    )
```
